512 devices in a mesh: seq: 32 (over x, z), tp: 16 (over y, core).
Axes of the slice: x: 4, y: 8, z: 8, core: 2. Of those that a mesh axis runs over, the one named last changes fastest.
Arguments:
- joined: bfloat16 [4096, 14336], P('seq', 'tp')
- gain: float32 [14336], P('tp'), may hold values from 0.25 to 1.75
- weight_codes: bfloat16 [7168, 14336], P('seq', 'tp'), may hold values from -0.046875 to 0.046875
- scale_exp: int32 [7168, 112], P('seq', 'tp'), may hold values from -2 to 1
- cotangent: bfloat16 [4096, 7168], P('tp', 'seq'), may hold values from -6 to 6
Outputs:
- projected: bfloat16 [4096, 7168], P('tp', 'seq')
- joined_gradient: bfloat16 [4096, 14336], P('seq', 'tp')
- weight_grad: float32 [7168, 14336], P('seq', 'tp')
The draws below stay inside these ranges and needn't reach their ends.
All inputs are finite; a program needn't handle non-finite values.
Results may differ from the reference program's by a relative error of at most 0.0057.
Values may be sent and summed in bfloat16 or wider, within the bound.
No kernel may reach another device: no remote copies, remote signals or barrier semaphores. Data moves between devices by JAX's collectives and lax.ppermute only.
A program may use at most 128 MiB of HBM per device.

```python
import jax
import jax.numpy as jnp
from jax import lax

MODEL_WIDTH = 7168
BLOCK = 128
TOKENS = 4096
N_SEQ = 32
N_TP = 16


def draw_joined(key, part):
    key = jax.random.fold_in(key, 3)
    key_rows, key_vals = jax.random.split(key, 2)
    columns = jnp.arange(2 * MODEL_WIDTH, dtype=jnp.float32)
    position = jnp.mod(columns, MODEL_WIDTH)
    col_scale = jnp.exp(jnp.log(3.0) * position / MODEL_WIDTH)
    row_scale = jnp.exp(jax.random.uniform(key_rows, (TOKENS, 1), jnp.float32, 0.0, jnp.log(10.0)))
    value_entries = jnp.clip(jax.random.normal(key_vals, (TOKENS, 2 * MODEL_WIDTH), jnp.float32), -4.0, 4.0)
    return (value_entries * col_scale[None, :] * row_scale).astype(jnp.bfloat16)


def place_ends(entries, own_key, low, largest):
    index_at = [jax.random.randint(jax.random.fold_in(own_key, axis), (), 0, length) for axis, length in enumerate(entries.shape)]
    widest = entries.shape.index(max(entries.shape))
    beside = index_at[:widest] + [(index_at[widest] + 1) % entries.shape[widest]] + index_at[widest + 1:]
    return entries.at[tuple(index_at)].set(low).at[tuple(beside)].set(largest)


def levels(stream_key, shape, cuts, low, largest):
    level, own = 1.0, jax.random.fold_in(stream_key, 6)
    for dim, parts in cuts:
        draws = jnp.exp(jax.random.uniform(jax.random.fold_in(own, dim), (parts,), jnp.float32, low / len(cuts), largest / len(cuts)))
        level = level * jnp.repeat(draws, shape[dim] // parts).reshape([-1 if axis == dim else 1 for axis in range(len(shape))])
    return level


def normal_values(stream_key, extent, spread, reach, cuts=(), kind=jnp.bfloat16):
    result = spread * jax.random.normal(stream_key, extent, jnp.float32)
    if cuts:
        result = result * levels(stream_key, extent, cuts, -0.22, 0.18)
    return jnp.clip(result, -reach, reach).astype(kind)


def setup_inputs(seed: int = 0) -> dict:
    seeds = jax.random.split(jax.random.key(seed), 6)
    return {
        "joined": draw_joined(jax.random.fold_in(seeds[5], 71), 0),
        "gain": jnp.clip(1.0 + 0.15 * jax.random.normal(seeds[1], (2 * MODEL_WIDTH,), jnp.float32), 0.25, 1.75),
        "weight_codes": normal_values(seeds[2], (MODEL_WIDTH, 2 * MODEL_WIDTH), (2 * MODEL_WIDTH) ** -0.5, 0.046875, ((0, 32), (1, 16))),
        "scale_exp": place_ends(jax.random.randint(seeds[3], (MODEL_WIDTH, 2 * MODEL_WIDTH // BLOCK), -2, 2), jax.random.fold_in(seeds[3], 1), -2, 1).astype(jnp.int32),
        "cotangent": normal_values(seeds[4], (TOKENS, MODEL_WIDTH), 1.0, 6.0, ((0, 16), (1, 32))),
    }


eps = 1e-06

def reference(joined, gain, weight_codes, scale_exp, cotangent):
    hidden_input = joined[:, :MODEL_WIDTH].astype(jnp.float32)
    embed_input = joined[:, MODEL_WIDTH:].astype(jnp.float32)
    hidden_reciprocal = lax.rsqrt(lax.optimization_barrier(jnp.mean(hidden_input * hidden_input, axis=1, keepdims=True)) + eps)
    embed_reciprocal = lax.rsqrt(lax.optimization_barrier(jnp.mean(embed_input * embed_input, axis=1, keepdims=True)) + eps)
    normalized_hidden = jnp.concatenate([hidden_input * hidden_reciprocal, embed_input * embed_reciprocal], axis=1)
    normalized_input = (normalized_hidden * gain[None, :]).astype(jnp.bfloat16)
    factor = jnp.repeat(jnp.exp2(scale_exp.astype(jnp.float32)), BLOCK, axis=1)
    weight = (weight_codes.astype(jnp.float32) * factor).astype(jnp.bfloat16)
    width_tp = 2 * MODEL_WIDTH // N_TP
    width_seq = MODEL_WIDTH // N_SEQ

    def forward_group(index, total):
        rows = lax.dynamic_slice_in_dim(normalized_input, index * width_tp, width_tp, 1)
        wcols = lax.dynamic_slice_in_dim(weight, index * width_tp, width_tp, 1)
        part = lax.dot_general(rows, wcols, (((1,), (1,)), ((), ())), preferred_element_type=jnp.float32).astype(jnp.bfloat16)
        return total + part.astype(jnp.float32)
    projected = lax.fori_loop(0, N_TP, forward_group, jnp.zeros((TOKENS, MODEL_WIDTH), jnp.float32)).astype(jnp.bfloat16)

    def backward_group(index, total):
        cols = lax.dynamic_slice_in_dim(cotangent, index * width_seq, width_seq, 1)
        wrows = lax.dynamic_slice_in_dim(weight, index * width_seq, width_seq, 0)
        part = jnp.dot(cols, wrows, preferred_element_type=jnp.float32).astype(jnp.bfloat16)
        return total + part.astype(jnp.float32)
    grad_normed = lax.fori_loop(0, N_SEQ, backward_group, jnp.zeros((TOKENS, 2 * MODEL_WIDTH), jnp.float32))
    upper_bound = grad_normed * gain[None, :]
    elementwise_product = upper_bound * normalized_hidden
    hidden_codes = lax.optimization_barrier(jnp.mean(elementwise_product[:, :MODEL_WIDTH], axis=1, keepdims=True))
    embed_codes = lax.optimization_barrier(jnp.mean(elementwise_product[:, MODEL_WIDTH:], axis=1, keepdims=True))
    hidden_gradient = hidden_reciprocal * (upper_bound[:, :MODEL_WIDTH] - normalized_hidden[:, :MODEL_WIDTH] * hidden_codes)
    embed_gradient = embed_reciprocal * (upper_bound[:, MODEL_WIDTH:] - normalized_hidden[:, MODEL_WIDTH:] * embed_codes)
    joined_gradient = jnp.concatenate([hidden_gradient, embed_gradient], axis=1).astype(jnp.bfloat16)
    weight_grad = lax.dot_general(cotangent, normalized_input, (((0,), (0,)), ((), ())), preferred_element_type=jnp.float32) / jnp.sqrt(jnp.float32(TOKENS))
    return (projected, joined_gradient, weight_grad)
```

```python
import jax
import jax.numpy as jnp
from jax import lax
from jax.experimental import pallas as pl
from jax.experimental.pallas import tpu as pltpu
from jax.sharding import Mesh, PartitionSpec as P

MODEL_WIDTH = 7168
BLOCK = 128
TOKENS = 4096
NX, NZ, NY, NC = 4, 8, 8, 2
ROWS = 128
FEATS = 224
COLS = 256
WIDTH = 896
eps = 1e-06
BF16, F32 = jnp.bfloat16, jnp.float32
VMEM = pl.BlockSpec(memory_space=pltpu.VMEM)
ANY = pl.BlockSpec(memory_space=pl.ANY)
PARAMS = pltpu.CompilerParams(vmem_limit_bytes=40 * 1024 * 1024)


def cost(flops, size):
    return pl.CostEstimate(flops=flops, bytes_accessed=size, transcendentals=0)


def row_scales(ss_ref):
    half = lax.axis_index("y") // (NY // 2)
    total = ss_ref[0]
    for p in range(1, 8):
        total = total + ss_ref[p]
    other = ss_ref[8]
    for p in range(9, 16):
        other = other + ss_ref[p]
    total = jnp.where(half == 0, total, other)
    return lax.rsqrt(total / MODEL_WIDTH + eps)


def input_grad_kernel(own, other, weight, grad, cot, sems):
    core = lax.axis_index("c")
    copies = []
    for m in range(8):
        for which, (block, parity) in enumerate(((own, core), (other, 1 - core))):
            start = pl.multiple_of(512 * (m % 2) + COLS * parity, COLS)
            copies.append(
                pltpu.make_async_copy(
                    block.at[m],
                    cot.at[pl.ds(FEATS * (m // 2), FEATS), pl.ds(start, COLS)],
                    sems.at[2 * m + which],
                )
            )
    for copy in copies:
        copy.start()
    for copy in copies:
        copy.wait()
    for j in range(4):
        part = lax.dot_general(
            cot[:, COLS * j : COLS * (j + 1)], weight[...], (((0,), (0,)), ((), ())), preferred_element_type=F32
        )
        grad[2 * j : 2 * j + 2] = part.astype(BF16).reshape(2, ROWS, WIDTH)


def forward_kernel(ss, joined, gain, weight, cot, normed, keep, send, dots):
    core = lax.axis_index("c")
    scales = row_scales(ss).T
    for z in range(NZ):
        value = joined[z].astype(F32) * scales[:, z : z + 1]
        normed[ROWS * z : ROWS * (z + 1), :] = (value * gain[...]).astype(BF16)
    for j in range(4):
        part = lax.dot_general(
            weight[...], normed[COLS * j : COLS * (j + 1), :], (((1,), (1,)), ((), ())), preferred_element_type=F32
        )
        dot = jnp.sum(part * cot[:, COLS * j : COLS * (j + 1)].astype(F32), axis=0, keepdims=True)
        dots[2 * j : 2 * j + 1, :] = dot[:, :ROWS]
        dots[2 * j + 1 : 2 * j + 2, :] = dot[:, ROWS:]
        part = part.astype(BF16)

        @pl.when(core == j % 2)
        def _():
            for i in range(4):
                keep[2 * i + j // 2] = part[FEATS * i : FEATS * (i + 1)]

        @pl.when(core != j % 2)
        def _():
            for i in range(4):
                send[2 * i + j // 2] = part[FEATS * i : FEATS * (i + 1)]


def weight_grad_kernel(cot, normed, out):
    for i in range(4):
        part = jnp.dot(cot[FEATS * i : FEATS * (i + 1), :], normed[...], preferred_element_type=F32)
        out[i] = (part * (1.0 / 64.0)).astype(BF16)


def joined_grad_kernel(ss, dots, grad, joined, gain, out):
    me = lax.axis_index("z")
    half = lax.axis_index("y") // (NY // 2)
    sums = jnp.sum(dots[...], axis=0)
    first = jnp.sum(sums[:8], axis=0, keepdims=True)
    second = jnp.sum(sums[8:], axis=0, keepdims=True)
    c = jnp.where(half == 0, first, second) / MODEL_WIDTH
    c = jnp.broadcast_to(c, (8, ROWS)).T[:, :1]
    scales = row_scales(ss)
    mine = lax.broadcasted_iota(jnp.int32, scales.shape, 0) == me
    scale = jnp.sum(jnp.where(mine, scales, 0.0), axis=0, keepdims=True)
    scale = jnp.broadcast_to(scale, (8, ROWS)).T[:, :1]
    u = grad[...].astype(F32) * gain[...]
    xhat = joined[...].astype(F32) * scale
    out[...] = (scale * (u - xhat * c)).astype(BF16)


def transposed():
    return [(x * NY + y, (y // 2) * NY + 2 * x + y % 2) for x in range(NX) for y in range(NY)]


def spread(value, count):
    return jnp.broadcast_to(value[None], (count,) + value.shape)


def per_device(joined, gain, weight_codes, scale_exp, cotangent):
    swap = [(0, 1), (1, 0)]
    gain = gain[None, :]
    joined_all = lax.all_gather(joined, "z")
    cot = lax.ppermute(cotangent.T, ("x", "y"), transposed())

    values = joined.astype(F32)
    squares = jnp.sum(values * values, axis=1)
    squares = lax.all_to_all(spread(squares, NZ), "z", 0, 0)
    squares = lax.all_to_all(spread(squares, NY * NC), ("y", "c"), 0, 0)

    factor = jnp.repeat(jnp.exp2(scale_exp.astype(F32)), BLOCK, axis=1)
    weight = (weight_codes.astype(F32) * factor).astype(BF16)
    weight = lax.all_to_all(spread(weight, NX), "x", 0, 0).reshape(NX * FEATS, WIDTH)

    own = lax.all_to_all(spread(cot, NY), "y", 0, 0)
    other = lax.ppermute(own, "c", swap)

    flops = 2 * 1024 * WIDTH * WIDTH
    grad, cot = pl.pallas_call(
        input_grad_kernel,
        out_shape=(jax.ShapeDtypeStruct((NZ, ROWS, WIDTH), BF16), jax.ShapeDtypeStruct((WIDTH, 1024), BF16)),
        in_specs=[ANY, ANY, VMEM],
        out_specs=(VMEM, VMEM),
        scratch_shapes=[pltpu.SemaphoreType.DMA((16,))],
        compiler_params=PARAMS,
        cost_estimate=cost(flops, 7 << 20),
        name="input_grad",
    )(own, other, weight)
    grad = lax.psum_scatter(grad, "z")

    normed, keep, send, dots = pl.pallas_call(
        forward_kernel,
        out_shape=(
            jax.ShapeDtypeStruct((1024, WIDTH), BF16),
            jax.ShapeDtypeStruct((8, FEATS, COLS), BF16),
            jax.ShapeDtypeStruct((8, FEATS, COLS), BF16),
            jax.ShapeDtypeStruct((NZ, ROWS), F32),
        ),
        in_specs=[VMEM] * 5,
        out_specs=(VMEM,) * 4,
        compiler_params=PARAMS,
        cost_estimate=cost(flops, 9 << 20),
        name="forward",
    )(squares, joined_all, gain, weight, cot)
    got = lax.ppermute(send, "c", swap)

    partial_wgrad = pl.pallas_call(
        weight_grad_kernel,
        out_shape=jax.ShapeDtypeStruct((NX, FEATS, WIDTH), BF16),
        in_specs=[VMEM, VMEM],
        out_specs=VMEM,
        compiler_params=PARAMS,
        cost_estimate=cost(flops, 6 << 20),
        name="weight_grad",
    )(cot, normed)

    both = (keep.astype(F32) + got.astype(F32)).astype(BF16)
    parts = lax.all_to_all(both, "y", 0, 0)
    projected = jnp.sum(parts.astype(F32), axis=0).astype(BF16)
    projected = lax.ppermute(projected, ("x", "y"), transposed()).T

    dots = jnp.broadcast_to(dots[:, None], (NZ, NY * NC, ROWS)).reshape(NZ * NY * NC, 1, ROWS)
    dots = lax.all_to_all(dots, ("z", "y", "c"), 0, 0).reshape(NZ, NY * NC, ROWS)

    wgrads = lax.all_to_all(partial_wgrad, "x", 0, 0)
    weight_grad = jnp.sum(wgrads.astype(F32), axis=0)

    joined_gradient = pl.pallas_call(
        joined_grad_kernel,
        out_shape=jax.ShapeDtypeStruct((ROWS, WIDTH), BF16),
        in_specs=[VMEM] * 5,
        out_specs=VMEM,
        compiler_params=PARAMS,
        cost_estimate=cost(8 * ROWS * WIDTH, 1 << 20),
        name="joined_grad",
    )(squares, dots, grad, joined, gain)
    return (projected, joined_gradient, weight_grad)


def solution(mesh):
    grid = Mesh(mesh.devices.reshape(NX, NZ, NY, NC), ("x", "z", "y", "c"))
    seq, tp = ("x", "z"), ("y", "c")
    in_specs = (P(seq, tp), P(tp), P(seq, tp), P(seq, tp), P(tp, seq))
    out_specs = (P(tp, seq), P(seq, tp), P(seq, tp))
    return jax.shard_map(per_device, mesh=grid, in_specs=in_specs, out_specs=out_specs, check_vma=False)
```

```python
import jax
import jax.numpy as jnp
from jax import lax
from jax.experimental import pallas as pl
from jax.experimental.pallas import tpu as pltpu
from jax.sharding import Mesh, PartitionSpec as P

MODEL_WIDTH = 7168
BLOCK = 128
TOKENS = 4096
NX, NZ, NY, NC = 4, 8, 8, 2
ROWS = 128
FEATS = 224
COLS = 256
WIDTH = 896
eps = 1e-06
BF16, F32 = jnp.bfloat16, jnp.float32
VMEM = pl.BlockSpec(memory_space=pltpu.VMEM)
ANY = pl.BlockSpec(memory_space=pl.ANY)
MIB = 1024 * 1024


def start_all(copies):
    for copy in copies:
        copy.start()
    return copies


def wait_all(copies):
    for copy in copies:
        copy.wait()


def weight_copies(blocks, weight, sems):
    x = lax.axis_index("x")
    copies = []
    for k, block in enumerate(blocks):
        start = pl.multiple_of(FEATS * lax.rem(x + NX - k, NX), 32)
        copies.append(pltpu.make_async_copy(block, weight.at[pl.ds(start, FEATS), :], sems.at[k]))
    return copies


def cot_copies(own, other, cot, sems):
    core = lax.axis_index("c")
    copies = []
    for m in range(8):
        for which, (block, parity) in enumerate(((own, core), (other, 1 - core))):
            start = pl.multiple_of(512 * (m % 2) + COLS * parity, COLS)
            place = cot.at[pl.ds(FEATS * (m // 2), FEATS), pl.ds(start, COLS)]
            copies.append(pltpu.make_async_copy(block.at[m], place, sems.at[4 + 2 * m + which]))
    return copies


def input_grad_kernel(own, other, w0, w1, w2, w3, grad, cot, weight, sems):
    wait_all(start_all(weight_copies((w0, w1, w2, w3), weight, sems) + cot_copies(own, other, cot, sems)))
    for j in range(4):
        part = lax.dot_general(
            cot[:, COLS * j : COLS * (j + 1)], weight[...], (((0,), (0,)), ((), ())), preferred_element_type=F32
        )
        grad[2 * j : 2 * j + 2] = part.astype(BF16).reshape(2, ROWS, WIDTH)


def forward_kernel(joined_in, gain, w0, w1, w2, w3, keep, send, squares, joined, weight, sems):
    core = lax.axis_index("c")
    copies = weight_copies((w0, w1, w2, w3), weight, sems)
    tokens = pltpu.make_async_copy(joined_in, joined, sems.at[4])
    start_all(copies + [tokens])
    wait_all(copies)
    weight[...] = (weight[...].astype(F32) * gain[...]).astype(BF16)
    tokens.wait()
    for j in range(4):
        rows = joined[2 * j : 2 * j + 2].reshape(COLS, WIDTH)
        part = lax.dot_general(
            weight[...], rows, (((1,), (1,)), ((), ())), preferred_element_type=F32
        ).astype(BF16)

        @pl.when(core == j % 2)
        def _():
            for i in range(4):
                keep[2 * i + j // 2] = part[FEATS * i : FEATS * (i + 1)]

        @pl.when(core != j % 2)
        def _():
            for i in range(4):
                send[2 * i + j // 2] = part[FEATS * i : FEATS * (i + 1)]

    lane = lax.broadcasted_iota(jnp.int32, (ROWS, ROWS), 1)
    sums = jnp.zeros((ROWS, ROWS), F32)
    for z in range(NZ):
        value = joined[z].astype(F32)
        sums = jnp.where(lane == z, jnp.sum(value * value, axis=1, keepdims=True), sums)
    squares[...] = sums.T[:NZ]


def project_kernel(ss, parts, out):
    j = 2 * lax.rem(lax.axis_index("y"), 2) + lax.axis_index("c")
    row = lax.broadcasted_iota(jnp.int32, (NZ, ROWS), 0)
    total = jnp.zeros((FEATS, COLS), F32)
    for half in range(2):
        scales = half_scales(ss, half)
        pair = [jnp.sum(jnp.where(row == 2 * j + i, scales, 0.0), axis=0, keepdims=True) for i in range(2)]
        part = parts[4 * half].astype(F32)
        for y in range(4 * half + 1, 4 * half + 4):
            part = part + parts[y].astype(F32)
        total = total + part * jnp.concatenate(pair, axis=1)
    out[...] = total.astype(BF16)


def weight_grad_kernel(ss, gain, own, other, joined_in, mine, o1, o2, o3, cot, joined, sems):
    x = lax.axis_index("x")
    copies = cot_copies(own, other, cot, sems)
    rows = pltpu.make_async_copy(joined_in, joined, sems.at[0])
    start_all(copies + [rows])
    scales = row_scales(ss)
    wait_all(copies)
    for z in range(NZ):
        part = cot[:, ROWS * z : ROWS * (z + 1)].astype(F32) * scales[z : z + 1]
        cot[:, ROWS * z : ROWS * (z + 1)] = part.astype(BF16)
    rows.wait()
    tokens = joined[...].reshape(NZ * ROWS, WIDTH)
    columns = gain[...] * (1.0 / 64.0)
    for k, out in enumerate((mine, o1, o2, o3)):
        start = pl.multiple_of(FEATS * lax.rem(x + k, NX), 32)
        part = jnp.dot(cot[pl.ds(start, FEATS), :], tokens, preferred_element_type=F32)
        out[...] = (part * columns).astype(out.dtype)


def half_scales(ss, half):
    return lax.rsqrt(ss[half] / MODEL_WIDTH + eps)


def row_scales(ss):
    return jnp.where(lax.axis_index("y") < NY // 2, half_scales(ss, 0), half_scales(ss, 1))


def column(row):
    return jnp.broadcast_to(row, (8, ROWS)).T[:, :1]


def own_scale(ss):
    scales = row_scales(ss)
    mine = lax.broadcasted_iota(jnp.int32, scales.shape, 0) == lax.axis_index("z")
    return column(jnp.sum(jnp.where(mine, scales, 0.0), axis=0, keepdims=True))


def dots_kernel(ss, grad, joined, gain, out):
    u = grad[...].astype(F32) * gain[...]
    xhat = joined[...].astype(F32) * own_scale(ss)
    dots = jnp.sum(u * xhat, axis=1, keepdims=True)
    out[...] = jnp.broadcast_to(dots, (ROWS, ROWS)).T[:1]


def joined_grad_kernel(ss, dots, grad, joined, gain, out):
    c = column(half_sum(dots[...]) / MODEL_WIDTH)
    scale = own_scale(ss)
    u = grad[...].astype(F32) * gain[...]
    xhat = joined[...].astype(F32) * scale
    out[...] = (scale * (u - xhat * c)).astype(BF16)


def half_sum(rows):
    first = jnp.sum(rows[:8], axis=0, keepdims=True)
    second = jnp.sum(rows[8:], axis=0, keepdims=True)
    return jnp.where(lax.axis_index("y") < NY // 2, first, second)


def over_tp(rows):
    return lax.all_to_all(jnp.broadcast_to(rows[None], (NY * NC,) + rows.shape), ("y", "c"), 0, 0)


def transposed():
    return [(x * NY + y, (y // 2) * NY + 2 * x + y % 2) for x in range(NX) for y in range(NY)]


def shifted(value, k):
    return lax.ppermute(value, "x", [(i, (i + k) % NX) for i in range(NX)])


def kernel(body, name, outs, flops, specs, out_specs=None, scratch=(), limit=40):
    return pl.pallas_call(
        body,
        out_shape=tuple(jax.ShapeDtypeStruct(shape, dtype) for shape, dtype in outs),
        in_specs=specs,
        out_specs=out_specs or (VMEM,) * len(outs),
        scratch_shapes=scratch,
        compiler_params=pltpu.CompilerParams(vmem_limit_bytes=limit * MIB),
        cost_estimate=pl.CostEstimate(flops=flops, bytes_accessed=6 << 20, transcendentals=0),
        name=name,
    )


def per_device(joined, gain, weight_codes, scale_exp, cotangent):
    swap = [(0, 1), (1, 0)]
    flops = 2 * 1024 * WIDTH * WIDTH
    bricks, square, blocks, block = (NZ, ROWS, WIDTH), (WIDTH, WIDTH), (8, FEATS, COLS), (FEATS, WIDTH)
    gain = gain[None, :]
    joined_all = lax.all_gather(joined, "z")
    cot = lax.ppermute(cotangent.T, ("x", "y"), transposed())

    factor = jnp.repeat(jnp.exp2(scale_exp.astype(F32)), BLOCK, axis=1)
    weight = (weight_codes.astype(F32) * factor).astype(BF16)
    weights = [weight] + [shifted(weight, k) for k in (1, 2, 3)]

    own = lax.all_gather(cot, "y")
    own, weights = lax.optimization_barrier((own, weights))
    other = lax.ppermute(own, "c", swap)

    scratch = [pltpu.VMEM((WIDTH, 1024), BF16), pltpu.VMEM(square, BF16), pltpu.VMEM(bricks, BF16), pltpu.SemaphoreType.DMA((21,))]
    (grad,) = kernel(
        input_grad_kernel,
        "input_grad",
        ((bricks, BF16),),
        flops,
        [ANY] * 6,
        scratch=[scratch[0], scratch[1], scratch[3]],
    )(own, other, *weights)
    grad = lax.psum_scatter(grad, "z")

    keep, send, squares = kernel(
        forward_kernel,
        "forward",
        ((blocks, BF16), (blocks, BF16), ((NZ, ROWS), F32)),
        flops,
        [ANY, VMEM, ANY, ANY, ANY, ANY],
        scratch=[scratch[2], scratch[1], scratch[3]],
    )(joined_all, gain, *weights)
    got = lax.ppermute(send, "c", swap)
    squares = over_tp(squares)
    squares = jnp.stack([jnp.sum(squares[:8], axis=0), jnp.sum(squares[8:], axis=0)])

    mine, *others = kernel(
        weight_grad_kernel,
        "weight_grad",
        ((block, F32), (block, BF16), (block, BF16), (block, BF16)),
        flops,
        [VMEM, VMEM, ANY, ANY, ANY],
        scratch=[scratch[0], scratch[2], scratch[3]],
    )(squares, gain, own, other, joined_all)
    others = [shifted(other, k + 1) for k, other in enumerate(others)]

    both = (keep.astype(F32) + got.astype(F32)).astype(BF16)
    both, squares = lax.optimization_barrier((both, squares))
    parts = lax.all_to_all(both, "y", 0, 0)
    (projected,) = kernel(project_kernel, "project", (((FEATS, COLS), BF16),), 16 * FEATS * COLS, [VMEM] * 2)(squares, parts)
    projected = lax.ppermute(projected, ("x", "y"), transposed()).T
    weight_grad = mine + others[0].astype(F32) + others[1].astype(F32) + others[2].astype(F32)

    (dots,) = kernel(dots_kernel, "dots", (((1, ROWS), F32),), 4 * ROWS * WIDTH, [VMEM] * 4)(squares, grad, joined, gain)
    dots = over_tp(dots).reshape(NY * NC, ROWS)
    (joined_gradient,) = kernel(
        joined_grad_kernel, "joined_grad", (((ROWS, WIDTH), BF16),), 8 * ROWS * WIDTH, [VMEM] * 5
    )(squares, dots, grad, joined, gain)
    return (projected, joined_gradient, weight_grad)


def solution(mesh):
    grid = Mesh(mesh.devices.reshape(NX, NZ, NY, NC), ("x", "z", "y", "c"))
    seq, tp = ("x", "z"), ("y", "c")
    in_specs = (P(seq, tp), P(tp), P(seq, tp), P(seq, tp), P(tp, seq))
    out_specs = (P(tp, seq), P(seq, tp), P(seq, tp))
    return jax.shard_map(per_device, mesh=grid, in_specs=in_specs, out_specs=out_specs, check_vma=False)
```

```python
import jax
import jax.numpy as jnp
from jax import lax
from jax.experimental import pallas as pl
from jax.experimental.pallas import tpu as pltpu
from jax.sharding import Mesh, PartitionSpec as P

MODEL_WIDTH = 7168
BLOCK = 128
TOKENS = 4096
NX, NZ, NY, NC = 4, 8, 8, 2
ROWS = 128
FEATS = 224
COLS = 256
WIDTH = 896
eps = 1e-06
BF16, F32 = jnp.bfloat16, jnp.float32
VMEM = pl.BlockSpec(memory_space=pltpu.VMEM)
ANY = pl.BlockSpec(memory_space=pl.ANY)
MIB = 1024 * 1024


def start_all(copies):
    for copy in copies:
        copy.start()
    return copies


def wait_all(copies):
    for copy in copies:
        copy.wait()


def cot_copies(own, other, cot, sems):
    core = lax.axis_index("c")
    copies = []
    for m in range(8):
        for which, (block, parity) in enumerate(((own, core), (other, 1 - core))):
            start = pl.multiple_of(512 * (m % 2) + COLS * parity, COLS)
            place = cot.at[pl.ds(FEATS * (m // 2), FEATS), pl.ds(start, COLS)]
            copies.append(pltpu.make_async_copy(block.at[m], place, sems.at[2 * m + which]))
    return copies


def input_grad_kernel(own, other, weight, grad, cot, sems):
    wait_all(start_all(cot_copies(own, other, cot, sems)))
    for j in range(4):
        part = lax.dot_general(
            cot[:, COLS * j : COLS * (j + 1)], weight[...], (((0,), (0,)), ((), ())), preferred_element_type=F32
        )
        grad[2 * j : 2 * j + 2] = part.astype(BF16).reshape(2, ROWS, WIDTH)


def forward_kernel(joined, gain, weight_in, keep, send, squares, weight):
    core = lax.axis_index("c")
    weight[...] = (weight_in[...].astype(F32) * gain[...]).astype(BF16)
    for j in range(4):
        rows = joined[2 * j : 2 * j + 2].reshape(COLS, WIDTH)
        part = lax.dot_general(
            weight[...], rows, (((1,), (1,)), ((), ())), preferred_element_type=F32
        ).astype(BF16)

        @pl.when(core == j % 2)
        def _():
            for i in range(4):
                keep[2 * i + j // 2] = part[FEATS * i : FEATS * (i + 1)]

        @pl.when(core != j % 2)
        def _():
            for i in range(4):
                send[2 * i + j // 2] = part[FEATS * i : FEATS * (i + 1)]

    lane = lax.broadcasted_iota(jnp.int32, (ROWS, ROWS), 1)
    sums = jnp.zeros((ROWS, ROWS), F32)
    for z in range(NZ):
        value = joined[z].astype(F32)
        sums = jnp.where(lane == z, jnp.sum(value * value, axis=1, keepdims=True), sums)
    squares[...] = sums.T[:NZ]


def scale_kernel(ss, keep, got, out):
    scales = row_scales(ss)
    row = lax.broadcasted_iota(jnp.int32, (NZ, ROWS), 0)
    for parity in range(2):
        j = 2 * parity + lax.axis_index("c")
        pair = [jnp.sum(jnp.where(row == 2 * j + i, scales, 0.0), axis=0, keepdims=True) for i in range(2)]
        scale = jnp.concatenate(pair, axis=1)
        for m in range(parity, 8, 2):
            out[m] = ((keep[m].astype(F32) + got[m].astype(F32)) * scale).astype(BF16)


def weight_grad_kernel(ss, gain, own, other, joined_in, mine, o1, o2, o3, cot, joined, sems):
    x = lax.axis_index("x")
    copies = cot_copies(own, other, cot, sems)
    rows = pltpu.make_async_copy(joined_in, joined, sems.at[16])
    start_all(copies + [rows])
    scales = row_scales(ss)
    wait_all(copies)
    for z in range(NZ):
        part = cot[:, ROWS * z : ROWS * (z + 1)].astype(F32) * scales[z : z + 1]
        cot[:, ROWS * z : ROWS * (z + 1)] = part.astype(BF16)
    rows.wait()
    tokens = joined[...].reshape(NZ * ROWS, WIDTH)
    columns = gain[...] * (1.0 / 64.0)
    for k, out in enumerate((mine, o1, o2, o3)):
        start = pl.multiple_of(FEATS * lax.rem(x + k, NX), 32)
        part = jnp.dot(cot[pl.ds(start, FEATS), :], tokens, preferred_element_type=F32)
        out[...] = (part * columns).astype(out.dtype)


def row_scales(ss):
    return lax.rsqrt(ss[...] / MODEL_WIDTH + eps)


def column(row):
    return jnp.broadcast_to(row, (8, ROWS)).T[:, :1]


def own_scale(ss):
    scales = row_scales(ss)
    mine = lax.broadcasted_iota(jnp.int32, scales.shape, 0) == lax.axis_index("z")
    return column(jnp.sum(jnp.where(mine, scales, 0.0), axis=0, keepdims=True))


def dots_kernel(ss, grad, joined, gain, out):
    u = grad[...].astype(F32) * gain[...]
    xhat = joined[...].astype(F32) * own_scale(ss)
    dots = jnp.sum(u * xhat, axis=1, keepdims=True)
    out[...] = jnp.broadcast_to(dots, (ROWS, ROWS)).T[:1]


def last_kernel(ss, dots, grad, joined, gain, mine, o1, o2, o3, out, weight_grad):
    weight_grad[...] = mine[...] + o1[...].astype(F32) + o2[...].astype(F32) + o3[...].astype(F32)
    c = column(dots[...] / MODEL_WIDTH)
    scale = own_scale(ss)
    u = grad[...].astype(F32) * gain[...]
    xhat = joined[...].astype(F32) * scale
    out[...] = (scale * (u - xhat * c)).astype(BF16)


def over_half(rows):
    groups = [list(range(8)), list(range(8, 16))]
    return lax.all_to_all(jnp.broadcast_to(rows[None], (8,) + rows.shape), ("y", "c"), 0, 0, axis_index_groups=groups)


def transposed():
    return [(x * NY + y, (y // 2) * NY + 2 * x + y % 2) for x in range(NX) for y in range(NY)]


def shifted(value, k):
    return lax.ppermute(value, "x", [(i, (i + k) % NX) for i in range(NX)])


def kernel(body, name, outs, flops, specs, out_specs=None, scratch=(), limit=40):
    return pl.pallas_call(
        body,
        out_shape=tuple(jax.ShapeDtypeStruct(shape, dtype) for shape, dtype in outs),
        in_specs=specs,
        out_specs=out_specs or (VMEM,) * len(outs),
        scratch_shapes=scratch,
        compiler_params=pltpu.CompilerParams(vmem_limit_bytes=limit * MIB),
        cost_estimate=pl.CostEstimate(flops=flops, bytes_accessed=6 << 20, transcendentals=0),
        name=name,
    )


def per_device(joined, gain, weight_codes, scale_exp, cotangent):
    swap = [(0, 1), (1, 0)]
    flops = 2 * 1024 * WIDTH * WIDTH
    bricks, square, blocks, block = (NZ, ROWS, WIDTH), (WIDTH, WIDTH), (8, FEATS, COLS), (FEATS, WIDTH)
    gain = gain[None, :]
    joined_all = lax.all_gather(joined, "z")
    cot = lax.ppermute(cotangent.T, ("x", "y"), transposed())

    factor = jnp.repeat(jnp.exp2(scale_exp.astype(F32)), BLOCK, axis=1)
    weight = (weight_codes.astype(F32) * factor).astype(BF16)
    weight = jnp.broadcast_to(weight[None], (NX, FEATS, WIDTH))
    weight = lax.all_to_all(weight, "x", 0, 0).reshape(square)

    own = lax.all_gather(cot, "y")
    other = lax.ppermute(own, "c", swap)

    scratch = [pltpu.VMEM((WIDTH, 1024), BF16), pltpu.VMEM(square, BF16), pltpu.VMEM(bricks, BF16), pltpu.SemaphoreType.DMA((17,))]
    (grad,) = kernel(
        input_grad_kernel,
        "input_grad",
        ((bricks, BF16),),
        flops,
        [ANY, ANY, VMEM],
        scratch=[scratch[0], scratch[3]],
    )(own, other, weight)
    grad = lax.psum_scatter(grad, "z")

    keep, send, squares = kernel(
        forward_kernel,
        "forward",
        ((blocks, BF16), (blocks, BF16), ((NZ, ROWS), F32)),
        flops,
        [VMEM] * 3,
        scratch=[scratch[1]],
    )(joined_all, gain, weight)
    got = lax.ppermute(send, "c", swap)
    squares = jnp.sum(over_half(squares), axis=0)

    mine, *others = kernel(
        weight_grad_kernel,
        "weight_grad",
        ((block, F32), (block, BF16), (block, BF16), (block, BF16)),
        flops,
        [VMEM, VMEM, ANY, ANY, ANY],
        scratch=[scratch[0], scratch[2], scratch[3]],
    )(squares, gain, own, other, joined_all)
    others = [shifted(other, k + 1) for k, other in enumerate(others)]

    (both,) = kernel(scale_kernel, "scale", ((blocks, BF16),), 4 * 8 * FEATS * COLS, [VMEM] * 3)(squares, keep, got)
    parts = lax.all_to_all(both, "y", 0, 0)
    projected = jnp.sum(parts.astype(F32), axis=0).astype(BF16)
    grad, projected = lax.optimization_barrier((grad, projected))
    (dots,) = kernel(dots_kernel, "dots", (((1, ROWS), F32),), 4 * ROWS * WIDTH, [VMEM] * 4)(squares, grad, joined, gain)
    projected = lax.ppermute(projected, ("x", "y"), transposed()).T
    dots = jnp.sum(over_half(dots), axis=0)
    joined_gradient, weight_grad = kernel(
        last_kernel, "last", (((ROWS, WIDTH), BF16), (block, F32)), 8 * ROWS * WIDTH, [VMEM] * 9
    )(squares, dots, grad, joined, gain, mine, *others)
    return (projected, joined_gradient, weight_grad)


def solution(mesh):
    grid = Mesh(mesh.devices.reshape(NX, NZ, NY, NC), ("x", "z", "y", "c"))
    seq, tp = ("x", "z"), ("y", "c")
    in_specs = (P(seq, tp), P(tp), P(seq, tp), P(seq, tp), P(tp, seq))
    out_specs = (P(tp, seq), P(seq, tp), P(seq, tp))
    return jax.shard_map(per_device, mesh=grid, in_specs=in_specs, out_specs=out_specs, check_vma=False)
```

```python
import jax
import jax.numpy as jnp
from jax import lax
from jax.experimental import pallas as pl
from jax.experimental.pallas import tpu as pltpu
from jax.sharding import Mesh, PartitionSpec as P

MODEL_WIDTH = 7168
BLOCK = 128
TOKENS = 4096
NX, NZ, NY, NC = 4, 8, 8, 2
ROWS = 128
FEATS = 224
COLS = 256
WIDTH = 896
eps = 1e-06
BF16, F32 = jnp.bfloat16, jnp.float32
VMEM = pl.BlockSpec(memory_space=pltpu.VMEM)
ANY = pl.BlockSpec(memory_space=pl.ANY)
MIB = 1024 * 1024


def start_all(copies):
    for copy in copies:
        copy.start()
    return copies


def wait_all(copies):
    for copy in copies:
        copy.wait()


def cot_copies(own, other, cot, sems):
    core = lax.axis_index("c")
    copies = []
    for m in range(8):
        for which, (block, parity) in enumerate(((own, core), (other, 1 - core))):
            start = pl.multiple_of(512 * (m % 2) + COLS * parity, COLS)
            place = cot.at[pl.ds(FEATS * (m // 2), FEATS), pl.ds(start, COLS)]
            copies.append(pltpu.make_async_copy(block.at[m], place, sems.at[2 * m + which]))
    return copies


def input_grad_kernel(own, other, weight, grad, cot, sems):
    wait_all(start_all(cot_copies(own, other, cot, sems)))
    for j in range(4):
        part = lax.dot_general(
            cot[:, COLS * j : COLS * (j + 1)], weight[...], (((0,), (0,)), ((), ())), preferred_element_type=F32
        )
        grad[2 * j : 2 * j + 2] = part.astype(BF16).reshape(2, ROWS, WIDTH)


def forward_kernel(joined, gain, weight_in, keep, send, squares, weight):
    core = lax.axis_index("c")
    weight[...] = (weight_in[...].astype(F32) * gain[...]).astype(BF16)
    rows = joined[...].reshape(NZ * ROWS, WIDTH)
    part = lax.dot_general(weight[...], rows, (((1,), (1,)), ((), ())), preferred_element_type=F32).astype(BF16)
    for j in range(4):
        columns = part[:, COLS * j : COLS * (j + 1)]

        @pl.when(core == j % 2)
        def _():
            for i in range(4):
                keep[2 * i + j // 2] = columns[FEATS * i : FEATS * (i + 1)]

        @pl.when(core != j % 2)
        def _():
            for i in range(4):
                send[2 * i + j // 2] = columns[FEATS * i : FEATS * (i + 1)]

    lane = lax.broadcasted_iota(jnp.int32, (ROWS, ROWS), 1)
    sums = jnp.zeros((ROWS, ROWS), F32)
    for z in range(NZ):
        value = joined[z].astype(F32)
        sums = jnp.where(lane == z, jnp.sum(value * value, axis=1, keepdims=True), sums)
    squares[...] = sums.T[:NZ]


def scale_kernel(ss, keep, got, out):
    scales = row_scales(ss)
    row = lax.broadcasted_iota(jnp.int32, (NZ, ROWS), 0)
    for parity in range(2):
        j = 2 * parity + lax.axis_index("c")
        pair = [jnp.sum(jnp.where(row == 2 * j + i, scales, 0.0), axis=0, keepdims=True) for i in range(2)]
        scale = jnp.concatenate(pair, axis=1)
        for m in range(parity, 8, 2):
            out[m] = ((keep[m].astype(F32) + got[m].astype(F32)) * scale).astype(BF16)


def weight_grad_kernel(ss, gain, own, other, joined_in, mine, o1, o2, o3, cot, joined, sems):
    x = lax.axis_index("x")
    copies = cot_copies(own, other, cot, sems)
    rows = pltpu.make_async_copy(joined_in, joined, sems.at[16])
    start_all(copies + [rows])
    scales = row_scales(ss)
    wait_all(copies)
    for z in range(NZ):
        part = cot[:, ROWS * z : ROWS * (z + 1)].astype(F32) * scales[z : z + 1]
        cot[:, ROWS * z : ROWS * (z + 1)] = part.astype(BF16)
    rows.wait()
    tokens = joined[...].reshape(NZ * ROWS, WIDTH)
    columns = gain[...] * (1.0 / 64.0)
    for k, out in enumerate((mine, o1, o2, o3)):
        start = pl.multiple_of(FEATS * lax.rem(x + k, NX), 32)
        part = jnp.dot(cot[pl.ds(start, FEATS), :], tokens, preferred_element_type=F32)
        out[...] = (part * columns).astype(out.dtype)


def row_scales(ss):
    return lax.rsqrt(ss[...] / MODEL_WIDTH + eps)


def column(row):
    return jnp.broadcast_to(row, (8, ROWS)).T[:, :1]


def own_scale(ss):
    scales = row_scales(ss)
    mine = lax.broadcasted_iota(jnp.int32, scales.shape, 0) == lax.axis_index("z")
    return column(jnp.sum(jnp.where(mine, scales, 0.0), axis=0, keepdims=True))


def dots_kernel(ss, grad, joined, gain, out, grad_out):
    grad_out[...] = grad[...]
    u = grad[...].astype(F32) * gain[...]
    xhat = joined[...].astype(F32) * own_scale(ss)
    dots = jnp.sum(u * xhat, axis=1, keepdims=True)
    out[...] = jnp.broadcast_to(dots, (ROWS, ROWS)).T[:1]


def last_kernel(ss, dots, grad, joined, gain, mine, o1, o2, o3, out, weight_grad):
    weight_grad[...] = mine[...] + o1[...].astype(F32) + o2[...].astype(F32) + o3[...].astype(F32)
    c = column(dots[...] / MODEL_WIDTH)
    scale = own_scale(ss)
    u = grad[...].astype(F32) * gain[...]
    xhat = joined[...].astype(F32) * scale
    out[...] = (scale * (u - xhat * c)).astype(BF16)


def over_half(rows):
    groups = [list(range(8)), list(range(8, 16))]
    return lax.all_to_all(jnp.broadcast_to(rows[None], (8,) + rows.shape), ("y", "c"), 0, 0, axis_index_groups=groups)


def transposed():
    return [(x * NY + y, (y // 2) * NY + 2 * x + y % 2) for x in range(NX) for y in range(NY)]


def shifted(value, k):
    return lax.ppermute(value, "x", [(i, (i + k) % NX) for i in range(NX)])


def kernel(body, name, outs, flops, specs, out_specs=None, scratch=(), limit=40):
    return pl.pallas_call(
        body,
        out_shape=tuple(jax.ShapeDtypeStruct(shape, dtype) for shape, dtype in outs),
        in_specs=specs,
        out_specs=out_specs or (VMEM,) * len(outs),
        scratch_shapes=scratch,
        compiler_params=pltpu.CompilerParams(vmem_limit_bytes=limit * MIB),
        cost_estimate=pl.CostEstimate(flops=flops, bytes_accessed=6 << 20, transcendentals=0),
        name=name,
    )


def per_device(joined, gain, weight_codes, scale_exp, cotangent):
    swap = [(0, 1), (1, 0)]
    flops = 2 * 1024 * WIDTH * WIDTH
    bricks, square, blocks, block = (NZ, ROWS, WIDTH), (WIDTH, WIDTH), (8, FEATS, COLS), (FEATS, WIDTH)
    gain = gain[None, :]
    joined_all = lax.all_gather(joined, "z")
    cot = lax.ppermute(cotangent.T, ("x", "y"), transposed())

    factor = jnp.repeat(jnp.exp2(scale_exp.astype(F32)), BLOCK, axis=1)
    weight = (weight_codes.astype(F32) * factor).astype(BF16)
    weight = jnp.broadcast_to(weight[None], (NX, FEATS, WIDTH))
    weight = lax.all_to_all(weight, "x", 0, 0).reshape(square)

    own = lax.all_gather(cot, "y")
    other = lax.ppermute(own, "c", swap)

    scratch = [pltpu.VMEM((WIDTH, 1024), BF16), pltpu.VMEM(square, BF16), pltpu.VMEM(bricks, BF16), pltpu.SemaphoreType.DMA((17,))]
    (grad,) = kernel(
        input_grad_kernel,
        "input_grad",
        ((bricks, BF16),),
        flops,
        [ANY, ANY, VMEM],
        scratch=[scratch[0], scratch[3]],
    )(own, other, weight)
    grad = lax.psum_scatter(grad, "z")

    keep, send, squares = kernel(
        forward_kernel,
        "forward",
        ((blocks, BF16), (blocks, BF16), ((NZ, ROWS), F32)),
        flops,
        [VMEM] * 3,
        scratch=[scratch[1]],
    )(joined_all, gain, weight)
    got = lax.ppermute(send, "c", swap)
    squares = jnp.sum(over_half(squares), axis=0)

    mine, *others = kernel(
        weight_grad_kernel,
        "weight_grad",
        ((block, F32), (block, BF16), (block, BF16), (block, BF16)),
        flops,
        [VMEM, VMEM, ANY, ANY, ANY],
        scratch=[scratch[0], scratch[2], scratch[3]],
    )(squares, gain, own, other, joined_all)
    others = [shifted(other, k + 1) for k, other in enumerate(others)]

    (both,) = kernel(scale_kernel, "scale", ((blocks, BF16),), 4 * 8 * FEATS * COLS, [VMEM] * 3)(squares, keep, got)
    parts = lax.all_to_all(both, "y", 0, 0)
    projected = jnp.sum(parts.astype(F32), axis=0).astype(BF16)
    grad, projected = lax.optimization_barrier((grad, projected))
    dots, grad = kernel(
        dots_kernel, "dots", (((1, ROWS), F32), ((ROWS, WIDTH), BF16)), 4 * ROWS * WIDTH, [VMEM] * 4
    )(squares, grad, joined, gain)
    projected = lax.ppermute(projected, ("x", "y"), transposed()).T
    dots = jnp.sum(over_half(dots), axis=0)
    joined_gradient, weight_grad = kernel(
        last_kernel, "last", (((ROWS, WIDTH), BF16), (block, F32)), 8 * ROWS * WIDTH, [VMEM] * 9
    )(squares, dots, grad, joined, gain, mine, *others)
    return (projected, joined_gradient, weight_grad)


def solution(mesh):
    grid = Mesh(mesh.devices.reshape(NX, NZ, NY, NC), ("x", "z", "y", "c"))
    seq, tp = ("x", "z"), ("y", "c")
    in_specs = (P(seq, tp), P(tp), P(seq, tp), P(seq, tp), P(tp, seq))
    out_specs = (P(tp, seq), P(seq, tp), P(seq, tp))
    return jax.shard_map(per_device, mesh=grid, in_specs=in_specs, out_specs=out_specs, check_vma=False)
```

```python
import jax
import jax.numpy as jnp
from jax import lax
from jax.experimental import pallas as pl
from jax.experimental.pallas import tpu as pltpu
from jax.sharding import Mesh, PartitionSpec as P

MODEL_WIDTH = 7168
BLOCK = 128
TOKENS = 4096
NX, NZ, NY, NC = 4, 8, 8, 2
ROWS = 128
FEATS = 224
COLS = 256
WIDTH = 896
eps = 1e-06
BF16, F32 = jnp.bfloat16, jnp.float32
VMEM = pl.BlockSpec(memory_space=pltpu.VMEM)
ANY = pl.BlockSpec(memory_space=pl.ANY)
MIB = 1024 * 1024


def scaled_weight_kernel(codes, exponents, out):
    factors = jnp.exp2(exponents[...].astype(F32))
    for b in range(WIDTH // BLOCK):
        columns = slice(BLOCK * b, BLOCK * (b + 1))
        part = (codes[:, columns].astype(F32) * factors[:, b : b + 1]).astype(BF16)
        for k in range(NX):
            out[k, :, columns] = part


def start_all(copies):
    for copy in copies:
        copy.start()
    return copies


def wait_all(copies):
    for copy in copies:
        copy.wait()


def cot_copies(own, other, cot, sems):
    core = lax.axis_index("c")
    copies = []
    for i in range(NX):
        for half in range(2):
            slot = traced_place(i, half)
            for which, (block, parity) in enumerate(((own, core), (other, 1 - core))):
                start = pl.multiple_of(512 * half + COLS * parity, COLS)
                place = cot.at[pl.ds(FEATS * i, FEATS), pl.ds(start, COLS)]
                copies.append(pltpu.make_async_copy(block.at[slot], place, sems.at[4 * i + 2 * half + which]))
    return copies


def input_grad_kernel(own, other, weight, grad, cot, sems):
    wait_all(start_all(cot_copies(own, other, cot, sems)))
    for j in range(4):
        part = lax.dot_general(
            cot[:, COLS * j : COLS * (j + 1)], weight[...], (((0,), (0,)), ((), ())), preferred_element_type=F32
        )
        grad[2 * j : 2 * j + 2] = part.astype(BF16).reshape(2, ROWS, WIDTH)


def forward_kernel(joined, gain, weight_in, keep, send, squares, weight):
    core = lax.axis_index("c")
    weight[...] = (weight_in[...].astype(F32) * gain[...]).astype(BF16)
    rows = joined[...].reshape(NZ * ROWS, WIDTH)
    part = lax.dot_general(weight[...], rows, (((1,), (1,)), ((), ())), preferred_element_type=F32).astype(BF16)
    for j in range(4):
        columns = part[:, COLS * j : COLS * (j + 1)]

        @pl.when(core == j % 2)
        def _():
            for i in range(4):
                keep[traced_place(i, j // 2)] = columns[FEATS * i : FEATS * (i + 1)]

        @pl.when(core != j % 2)
        def _():
            for i in range(4):
                send[traced_place(i, j // 2)] = columns[FEATS * i : FEATS * (i + 1)]

    lane = lax.broadcasted_iota(jnp.int32, (ROWS, ROWS), 1)
    sums = jnp.zeros((ROWS, ROWS), F32)
    for z in range(NZ):
        value = joined[z].astype(F32)
        sums = jnp.where(lane == z, jnp.sum(value * value, axis=1, keepdims=True), sums)
    squares[...] = jnp.broadcast_to(sums.T[None, :NZ], (8, NZ, ROWS))


def scale_kernel(ss, keep, got, out):
    scales = row_scales(ss)
    row = lax.broadcasted_iota(jnp.int32, (NZ, ROWS), 0)
    for parity in range(2):
        j = 2 * parity + lax.axis_index("c")
        pair = [jnp.sum(jnp.where(row == 2 * j + i, scales, 0.0), axis=0, keepdims=True) for i in range(2)]
        scale = jnp.concatenate(pair, axis=1)
        for i in range(NX):
            m = traced_place(i, parity)
            out[m] = ((keep[m].astype(F32) + got[m].astype(F32)) * scale).astype(BF16)


def weight_grad_kernel(ss, gain, own, other, joined_in, mine, o1, o2, o3, cot, joined, sems):
    x = lax.axis_index("x")
    copies = cot_copies(own, other, cot, sems)
    rows = pltpu.make_async_copy(joined_in, joined, sems.at[16])
    start_all(copies + [rows])
    scales = row_scales(ss)
    wait_all(copies)
    for z in range(NZ):
        part = cot[:, ROWS * z : ROWS * (z + 1)].astype(F32) * scales[z : z + 1]
        cot[:, ROWS * z : ROWS * (z + 1)] = part.astype(BF16)
    rows.wait()
    tokens = joined[...].reshape(NZ * ROWS, WIDTH)
    columns = gain[...] * (1.0 / 64.0)
    for k, out in enumerate((mine, o1, o2, o3)):
        start = pl.multiple_of(FEATS * lax.rem(x + k, NX), 32)
        part = jnp.dot(cot[pl.ds(start, FEATS), :], tokens, preferred_element_type=F32)
        out[...] = (part * columns).astype(out.dtype)


def row_scales(ss):
    return lax.rsqrt(jnp.sum(ss[...], axis=0) / MODEL_WIDTH + eps)


def column(row):
    return jnp.broadcast_to(row, (8, ROWS)).T[:, :1]


def own_scale(ss):
    scales = row_scales(ss)
    mine = lax.broadcasted_iota(jnp.int32, scales.shape, 0) == lax.axis_index("z")
    return column(jnp.sum(jnp.where(mine, scales, 0.0), axis=0, keepdims=True))


def dots_kernel(ss, grad, joined, gain, out, grad_out):
    grad_out[...] = grad[...]
    u = grad[...].astype(F32) * gain[...]
    xhat = joined[...].astype(F32) * own_scale(ss)
    dots = jnp.sum(u * xhat, axis=1, keepdims=True)
    out[...] = jnp.broadcast_to(jnp.broadcast_to(dots, (ROWS, ROWS)).T[None, :1], (8, 1, ROWS))


def last_kernel(ss, dots, grad, joined, gain, mine, o1, o2, o3, projected_in, out, weight_grad, projected):
    projected[...] = projected_in[...]
    weight_grad[...] = mine[...] + o1[...].astype(F32) + o2[...].astype(F32) + o3[...].astype(F32)
    c = column(jnp.sum(dots[...], axis=0) / MODEL_WIDTH)
    scale = own_scale(ss)
    u = grad[...].astype(F32) * gain[...]
    xhat = joined[...].astype(F32) * scale
    out[...] = (scale * (u - xhat * c)).astype(BF16)


def over_half(copies):
    groups = [list(range(8)), list(range(8, 16))]
    return lax.all_to_all(copies, ("y", "c"), 0, 0, axis_index_groups=groups)


def meeting_place(x, source, parity):
    away = (source + NX - x) % NX
    along = (3, 2, 0, 1)[away]
    return (2 * x + 1 + along) % NY if parity else (2 * x + NY - along) % NY


def to_meeting_place():
    return [
        (source * NY + y, (y // 2) * NY + meeting_place(y // 2, source, y % 2)) for source in range(NX) for y in range(NY)
    ]


def traced_place(source, parity):
    x = lax.axis_index("x")
    away = lax.rem(source + NX - x, NX)
    along = jnp.where(away == 0, 3, jnp.where(away == 1, 2, jnp.where(away == 2, 0, 1)))
    return lax.rem(2 * x + 1 + along, NY) if parity else lax.rem(2 * x + NY - along, NY)


def shifted(value, k):
    return lax.ppermute(value, "x", [(i, (i + k) % NX) for i in range(NX)])


def kernel(body, name, outs, flops, specs, out_specs=None, scratch=(), limit=40):
    return pl.pallas_call(
        body,
        out_shape=tuple(jax.ShapeDtypeStruct(shape, dtype) for shape, dtype in outs),
        in_specs=specs,
        out_specs=out_specs or (VMEM,) * len(outs),
        scratch_shapes=scratch,
        compiler_params=pltpu.CompilerParams(vmem_limit_bytes=limit * MIB),
        cost_estimate=pl.CostEstimate(flops=flops, bytes_accessed=6 << 20, transcendentals=0),
        name=name,
    )


def per_device(joined, gain, weight_codes, scale_exp, cotangent):
    swap = [(0, 1), (1, 0)]
    flops = 2 * 1024 * WIDTH * WIDTH
    bricks, square, blocks, block = (NZ, ROWS, WIDTH), (WIDTH, WIDTH), (8, FEATS, COLS), (FEATS, WIDTH)
    gain = gain[None, :]
    joined_all = lax.all_gather(joined, "z")
    cot = lax.ppermute(cotangent.T, ("x", "y"), to_meeting_place())

    (weight,) = kernel(
        scaled_weight_kernel, "scaled_weight", (((NX,) + block, BF16),), 4 * FEATS * WIDTH, [VMEM] * 2
    )(weight_codes, scale_exp)
    weight = lax.all_to_all(weight, "x", 0, 0).reshape(square)

    own = lax.all_gather(cot, "y")
    other = lax.ppermute(own, "c", swap)

    scratch = [pltpu.VMEM((WIDTH, 1024), BF16), pltpu.VMEM(square, BF16), pltpu.VMEM(bricks, BF16), pltpu.SemaphoreType.DMA((17,))]
    (grad,) = kernel(
        input_grad_kernel,
        "input_grad",
        ((bricks, BF16),),
        flops,
        [ANY, ANY, VMEM],
        scratch=[scratch[0], scratch[3]],
    )(own, other, weight)
    grad = lax.psum_scatter(grad, "z")

    keep, send, squares = kernel(
        forward_kernel,
        "forward",
        ((blocks, BF16), (blocks, BF16), ((8, NZ, ROWS), F32)),
        flops,
        [VMEM] * 3,
        scratch=[scratch[1]],
    )(joined_all, gain, weight)
    got = lax.ppermute(send, "c", swap)
    squares = over_half(squares)

    mine, *others = kernel(
        weight_grad_kernel,
        "weight_grad",
        ((block, F32), (block, BF16), (block, BF16), (block, BF16)),
        flops,
        [VMEM, VMEM, ANY, ANY, ANY],
        scratch=[scratch[0], scratch[2], scratch[3]],
    )(squares, gain, own, other, joined_all)
    others = [shifted(other, k + 1) for k, other in enumerate(others)]

    (both,) = kernel(scale_kernel, "scale", ((blocks, BF16),), 4 * 8 * FEATS * COLS, [VMEM] * 3)(squares, keep, got)
    parts = lax.all_to_all(both, "y", 0, 0)
    projected = jnp.sum(parts.astype(F32), axis=0).astype(BF16)
    grad, projected = lax.optimization_barrier((grad, projected))
    dots, grad = kernel(
        dots_kernel, "dots", (((8, 1, ROWS), F32), ((ROWS, WIDTH), BF16)), 4 * ROWS * WIDTH, [VMEM] * 4
    )(squares, grad, joined, gain)
    projected = lax.ppermute(projected, ("x", "y"), [(b, a) for a, b in to_meeting_place()])
    dots = over_half(dots)
    joined_gradient, weight_grad, projected = kernel(
        last_kernel,
        "last",
        (((ROWS, WIDTH), BF16), (block, F32), ((FEATS, COLS), BF16)),
        8 * ROWS * WIDTH,
        [VMEM] * 10,
    )(squares, dots, grad, joined, gain, mine, *others, projected)
    return (projected.T, joined_gradient, weight_grad)


def solution(mesh):
    grid = Mesh(mesh.devices.reshape(NX, NZ, NY, NC), ("x", "z", "y", "c"))
    seq, tp = ("x", "z"), ("y", "c")
    in_specs = (P(seq, tp), P(tp), P(seq, tp), P(seq, tp), P(tp, seq))
    out_specs = (P(tp, seq), P(seq, tp), P(seq, tp))
    return jax.shard_map(per_device, mesh=grid, in_specs=in_specs, out_specs=out_specs, check_vma=False)
```

```python
import jax
import jax.numpy as jnp
from jax import lax
from jax.experimental import pallas as pl
from jax.experimental.pallas import tpu as pltpu
from jax.sharding import Mesh, PartitionSpec as P

MODEL_WIDTH = 7168
BLOCK = 128
TOKENS = 4096
NX, NZ, NY, NC = 4, 8, 8, 2
ROWS = 128
FEATS = 224
COLS = 256
WIDTH = 896
eps = 1e-06
BF16, F32 = jnp.bfloat16, jnp.float32
VMEM = pl.BlockSpec(memory_space=pltpu.VMEM)
ANY = pl.BlockSpec(memory_space=pl.ANY)
MIB = 1024 * 1024


def scaled_weight_kernel(codes, exponents, out):
    factors = jnp.exp2(exponents[...].astype(F32))
    for b in range(WIDTH // BLOCK):
        columns = slice(BLOCK * b, BLOCK * (b + 1))
        part = (codes[:, columns].astype(F32) * factors[:, b : b + 1]).astype(BF16)
        for k in range(NX):
            out[k, :, columns] = part


def start_all(copies):
    for copy in copies:
        copy.start()
    return copies


def wait_all(copies):
    for copy in copies:
        copy.wait()


def cot_copies(own, other, cot, sems):
    core = lax.axis_index("c")
    copies = []
    for m in range(8):
        for which, (block, parity) in enumerate(((own, core), (other, 1 - core))):
            start = pl.multiple_of(512 * (m % 2) + COLS * parity, COLS)
            place = cot.at[pl.ds(FEATS * (m // 2), FEATS), pl.ds(start, COLS)]
            copies.append(pltpu.make_async_copy(block.at[m], place, sems.at[2 * m + which]))
    return copies


def input_grad_kernel(own, other, weight, grad, cot, sems):
    wait_all(start_all(cot_copies(own, other, cot, sems)))
    for j in range(4):
        part = lax.dot_general(
            cot[:, COLS * j : COLS * (j + 1)], weight[...], (((0,), (0,)), ((), ())), preferred_element_type=F32
        )
        grad[2 * j : 2 * j + 2] = part.astype(BF16).reshape(2, ROWS, WIDTH)


def forward_kernel(joined, gain, weight_in, keep, send, squares, weight):
    core = lax.axis_index("c")
    weight[...] = (weight_in[...].astype(F32) * gain[...]).astype(BF16)
    rows = joined[...].reshape(NZ * ROWS, WIDTH)
    part = lax.dot_general(weight[...], rows, (((1,), (1,)), ((), ())), preferred_element_type=F32).astype(BF16)
    for j in range(4):
        columns = part[:, COLS * j : COLS * (j + 1)]

        @pl.when(core == j % 2)
        def _():
            for i in range(4):
                keep[2 * i + j // 2] = columns[FEATS * i : FEATS * (i + 1)]

        @pl.when(core != j % 2)
        def _():
            for i in range(4):
                send[2 * i + j // 2] = columns[FEATS * i : FEATS * (i + 1)]

    lane = lax.broadcasted_iota(jnp.int32, (ROWS, ROWS), 1)
    sums = jnp.zeros((ROWS, ROWS), F32)
    for z in range(NZ):
        value = joined[z].astype(F32)
        sums = jnp.where(lane == z, jnp.sum(value * value, axis=1, keepdims=True), sums)
    squares[...] = jnp.broadcast_to(sums.T[None, :NZ], (8, NZ, ROWS))


def scale_kernel(ss, keep, got, out):
    scales = row_scales(ss)
    row = lax.broadcasted_iota(jnp.int32, (NZ, ROWS), 0)
    for parity in range(2):
        j = 2 * parity + lax.axis_index("c")
        pair = [jnp.sum(jnp.where(row == 2 * j + i, scales, 0.0), axis=0, keepdims=True) for i in range(2)]
        scale = jnp.concatenate(pair, axis=1)
        for m in range(parity, 8, 2):
            out[m] = ((keep[m].astype(F32) + got[m].astype(F32)) * scale).astype(BF16)


def weight_grad_kernel(ss, gain, own, other, joined_in, mine, o1, o2, o3, cot, joined, sems):
    x = lax.axis_index("x")
    copies = cot_copies(own, other, cot, sems)
    rows = pltpu.make_async_copy(joined_in, joined, sems.at[16])
    start_all(copies + [rows])
    scales = row_scales(ss)
    wait_all(copies)
    for z in range(NZ):
        part = cot[:, ROWS * z : ROWS * (z + 1)].astype(F32) * scales[z : z + 1]
        cot[:, ROWS * z : ROWS * (z + 1)] = part.astype(BF16)
    rows.wait()
    tokens = joined[...].reshape(NZ * ROWS, WIDTH)
    columns = gain[...] * (1.0 / 64.0)
    for k, out in enumerate((mine, o1, o2, o3)):
        start = pl.multiple_of(FEATS * lax.rem(x + k, NX), 32)
        part = jnp.dot(cot[pl.ds(start, FEATS), :], tokens, preferred_element_type=F32)
        out[...] = (part * columns).astype(out.dtype)


def row_scales(ss):
    return lax.rsqrt(jnp.sum(ss[...], axis=0) / MODEL_WIDTH + eps)


def column(row):
    return jnp.broadcast_to(row, (8, ROWS)).T[:, :1]


def own_scale(ss):
    scales = row_scales(ss)
    mine = lax.broadcasted_iota(jnp.int32, scales.shape, 0) == lax.axis_index("z")
    return column(jnp.sum(jnp.where(mine, scales, 0.0), axis=0, keepdims=True))


def dots_kernel(ss, grad, joined, gain, out, grad_out):
    grad_out[...] = grad[...]
    u = grad[...].astype(F32) * gain[...]
    xhat = joined[...].astype(F32) * own_scale(ss)
    dots = jnp.sum(u * xhat, axis=1, keepdims=True)
    out[...] = jnp.broadcast_to(jnp.broadcast_to(dots, (ROWS, ROWS)).T[None, :1], (8, 1, ROWS))


def last_kernel(ss, dots, grad, joined, gain, mine, o1, o2, o3, projected_in, out, weight_grad, projected):
    projected[...] = projected_in[...]
    weight_grad[...] = mine[...] + o1[...].astype(F32) + o2[...].astype(F32) + o3[...].astype(F32)
    c = column(jnp.sum(dots[...], axis=0) / MODEL_WIDTH)
    scale = own_scale(ss)
    u = grad[...].astype(F32) * gain[...]
    xhat = joined[...].astype(F32) * scale
    out[...] = (scale * (u - xhat * c)).astype(BF16)


def over_half(copies):
    groups = [list(range(8)), list(range(8, 16))]
    return lax.all_to_all(copies, ("y", "c"), 0, 0, axis_index_groups=groups)


def transposed():
    return [(x * NY + y, (y // 2) * NY + 2 * x + y % 2) for x in range(NX) for y in range(NY)]


def shifted(value, k):
    return lax.ppermute(value, "x", [(i, (i + k) % NX) for i in range(NX)])


def kernel(body, name, outs, flops, specs, out_specs=None, scratch=(), limit=40):
    return pl.pallas_call(
        body,
        out_shape=tuple(jax.ShapeDtypeStruct(shape, dtype) for shape, dtype in outs),
        in_specs=specs,
        out_specs=out_specs or (VMEM,) * len(outs),
        scratch_shapes=scratch,
        compiler_params=pltpu.CompilerParams(vmem_limit_bytes=limit * MIB),
        cost_estimate=pl.CostEstimate(flops=flops, bytes_accessed=6 << 20, transcendentals=0),
        name=name,
    )


def per_device(joined, gain, weight_codes, scale_exp, cotangent):
    swap = [(0, 1), (1, 0)]
    flops = 2 * 1024 * WIDTH * WIDTH
    bricks, square, blocks, block = (NZ, ROWS, WIDTH), (WIDTH, WIDTH), (8, FEATS, COLS), (FEATS, WIDTH)
    gain = gain[None, :]
    joined_all = lax.all_gather(joined, "z")
    cot = lax.ppermute(cotangent.T, ("x", "y"), transposed())

    (weight,) = kernel(
        scaled_weight_kernel, "scaled_weight", (((NX,) + block, BF16),), 4 * FEATS * WIDTH, [VMEM] * 2
    )(weight_codes, scale_exp)
    weight = lax.all_to_all(weight, "x", 0, 0).reshape(square)

    own = lax.all_gather(cot, "y")
    other = lax.ppermute(own, "c", swap)

    scratch = [pltpu.VMEM((WIDTH, 1024), BF16), pltpu.VMEM(square, BF16), pltpu.VMEM(bricks, BF16), pltpu.SemaphoreType.DMA((17,))]
    (grad,) = kernel(
        input_grad_kernel,
        "input_grad",
        ((bricks, BF16),),
        flops,
        [ANY, ANY, VMEM],
        scratch=[scratch[0], scratch[3]],
    )(own, other, weight)
    grad = lax.psum_scatter(grad, "z")

    keep, send, squares = kernel(
        forward_kernel,
        "forward",
        ((blocks, BF16), (blocks, BF16), ((8, NZ, ROWS), F32)),
        flops,
        [VMEM] * 3,
        scratch=[scratch[1]],
    )(joined_all, gain, weight)
    got = lax.ppermute(send, "c", swap)
    squares = over_half(squares)

    mine, *others = kernel(
        weight_grad_kernel,
        "weight_grad",
        ((block, F32), (block, BF16), (block, BF16), (block, BF16)),
        flops,
        [VMEM, VMEM, ANY, ANY, ANY],
        scratch=[scratch[0], scratch[2], scratch[3]],
    )(squares, gain, own, other, joined_all)
    others = [shifted(other, k + 1) for k, other in enumerate(others)]

    (both,) = kernel(scale_kernel, "scale", ((blocks, BF16),), 4 * 8 * FEATS * COLS, [VMEM] * 3)(squares, keep, got)
    parts = lax.all_to_all(both, "y", 0, 0)
    projected = jnp.sum(parts.astype(F32), axis=0).astype(BF16)
    grad, projected = lax.optimization_barrier((grad, projected))
    dots, grad = kernel(
        dots_kernel, "dots", (((8, 1, ROWS), F32), ((ROWS, WIDTH), BF16)), 4 * ROWS * WIDTH, [VMEM] * 4
    )(squares, grad, joined, gain)
    projected = lax.ppermute(projected, ("x", "y"), transposed())
    dots = over_half(dots)
    joined_gradient, weight_grad, projected = kernel(
        last_kernel,
        "last",
        (((ROWS, WIDTH), BF16), (block, F32), ((FEATS, COLS), BF16)),
        8 * ROWS * WIDTH,
        [VMEM] * 10,
    )(squares, dots, grad, joined, gain, mine, *others, projected)
    return (projected.T, joined_gradient, weight_grad)


def solution(mesh):
    grid = Mesh(mesh.devices.reshape(NX, NZ, NY, NC), ("x", "z", "y", "c"))
    seq, tp = ("x", "z"), ("y", "c")
    in_specs = (P(seq, tp), P(tp), P(seq, tp), P(seq, tp), P(tp, seq))
    out_specs = (P(tp, seq), P(seq, tp), P(seq, tp))
    return jax.shard_map(per_device, mesh=grid, in_specs=in_specs, out_specs=out_specs, check_vma=False)
```

```python
import jax
import jax.numpy as jnp
from jax import lax
from jax.experimental import pallas as pl
from jax.experimental.pallas import tpu as pltpu
from jax.sharding import Mesh, PartitionSpec as P

MODEL_WIDTH = 7168
BLOCK = 128
TOKENS = 4096
NX, NZ, NY, NC = 4, 8, 8, 2
ROWS = 128
FEATS = 224
COLS = 256
WIDTH = 896
eps = 1e-06
BF16, F32 = jnp.bfloat16, jnp.float32
VMEM = pl.BlockSpec(memory_space=pltpu.VMEM)
ANY = pl.BlockSpec(memory_space=pl.ANY)
MIB = 1024 * 1024


def scaled_weight_kernel(codes, exponents, out):
    factors = jnp.exp2(exponents[...].astype(F32))
    for b in range(WIDTH // BLOCK):
        columns = slice(BLOCK * b, BLOCK * (b + 1))
        part = (codes[:, columns].astype(F32) * factors[:, b : b + 1]).astype(BF16)
        for k in range(NX):
            out[k, :, columns] = part


def start_all(copies):
    for copy in copies:
        copy.start()
    return copies


def wait_all(copies):
    for copy in copies:
        copy.wait()


def cot_copies(own, other, cot, sems):
    core = lax.axis_index("c")
    copies = []
    for m in range(8):
        for which, (block, parity) in enumerate(((own, core), (other, 1 - core))):
            start = pl.multiple_of(512 * (m % 2) + COLS * parity, COLS)
            place = cot.at[pl.ds(FEATS * (m // 2), FEATS), pl.ds(start, COLS)]
            copies.append(pltpu.make_async_copy(block.at[m], place, sems.at[2 * m + which]))
    return copies


def input_grad_kernel(own, other, weight, gain, grad, cot, sems):
    wait_all(start_all(cot_copies(own, other, cot, sems)))
    for j in range(4):
        part = lax.dot_general(
            cot[:, COLS * j : COLS * (j + 1)], weight[...], (((0,), (0,)), ((), ())), preferred_element_type=F32
        )
        grad[2 * j : 2 * j + 2] = part.astype(BF16).reshape(2, ROWS, WIDTH)


def forward_kernel(joined, gain, weight_in, keep, send, squares, weight):
    core = lax.axis_index("c")
    weight[...] = (weight_in[...].astype(F32) * gain[...]).astype(BF16)
    rows = joined[...].reshape(NZ * ROWS, WIDTH)
    part = lax.dot_general(weight[...], rows, (((1,), (1,)), ((), ())), preferred_element_type=F32).astype(BF16)
    for j in range(4):
        columns = part[:, COLS * j : COLS * (j + 1)]

        @pl.when(core == j % 2)
        def _():
            for i in range(4):
                keep[2 * i + j // 2] = columns[FEATS * i : FEATS * (i + 1)]

        @pl.when(core != j % 2)
        def _():
            for i in range(4):
                send[2 * i + j // 2] = columns[FEATS * i : FEATS * (i + 1)]

    lane = lax.broadcasted_iota(jnp.int32, (ROWS, ROWS), 1)
    sums = jnp.zeros((ROWS, ROWS), F32)
    for z in range(NZ):
        value = joined[z].astype(F32)
        sums = jnp.where(lane == z, jnp.sum(value * value, axis=1, keepdims=True), sums)
    squares[...] = jnp.broadcast_to(sums.T[None, :NZ], (8, NZ, ROWS))


def scale_kernel(ss, keep, got, out):
    scales = row_scales(ss)
    row = lax.broadcasted_iota(jnp.int32, (NZ, ROWS), 0)
    for parity in range(2):
        j = 2 * parity + lax.axis_index("c")
        pair = [jnp.sum(jnp.where(row == 2 * j + i, scales, 0.0), axis=0, keepdims=True) for i in range(2)]
        scale = jnp.concatenate(pair, axis=1)
        for m in range(parity, 8, 2):
            out[m] = ((keep[m].astype(F32) + got[m].astype(F32)) * scale).astype(BF16)


def weight_grad_kernel(ss, gain, own, other, joined_in, mine, o1, o2, o3, cot, joined, sems):
    x = lax.axis_index("x")
    copies = cot_copies(own, other, cot, sems)
    rows = pltpu.make_async_copy(joined_in, joined, sems.at[16])
    start_all(copies + [rows])
    scales = row_scales(ss)
    wait_all(copies)
    for z in range(NZ):
        part = cot[:, ROWS * z : ROWS * (z + 1)].astype(F32) * scales[z : z + 1]
        cot[:, ROWS * z : ROWS * (z + 1)] = part.astype(BF16)
    rows.wait()
    tokens = joined[...].reshape(NZ * ROWS, WIDTH)
    columns = gain[...] * (1.0 / 64.0)
    for k, out in enumerate((mine, o1, o2, o3)):
        start = pl.multiple_of(FEATS * lax.rem(x + k, NX), 32)
        part = jnp.dot(cot[pl.ds(start, FEATS), :], tokens, preferred_element_type=F32)
        out[...] = (part * columns).astype(out.dtype)


def row_scales(ss):
    return lax.rsqrt(jnp.sum(ss[...], axis=0) / MODEL_WIDTH + eps)


def column(row):
    return jnp.broadcast_to(row, (8, ROWS)).T[:, :1]


def own_scale(ss):
    scales = row_scales(ss)
    mine = lax.broadcasted_iota(jnp.int32, scales.shape, 0) == lax.axis_index("z")
    return column(jnp.sum(jnp.where(mine, scales, 0.0), axis=0, keepdims=True))


def dots_kernel(ss, grad, joined, gain, out, grad_out):
    grad_out[...] = grad[...]
    u = grad[...].astype(F32) * gain[...]
    xhat = joined[...].astype(F32) * own_scale(ss)
    dots = jnp.sum(u * xhat, axis=1, keepdims=True)
    out[...] = jnp.broadcast_to(jnp.broadcast_to(dots, (ROWS, ROWS)).T[None, :1], (8, 1, ROWS))


def last_kernel(ss, dots, grad, joined, gain, mine, o1, o2, o3, projected_in, out, weight_grad, projected):
    projected[...] = projected_in[...]
    weight_grad[...] = mine[...] + o1[...].astype(F32) + o2[...].astype(F32) + o3[...].astype(F32)
    c = column(jnp.sum(dots[...], axis=0) / MODEL_WIDTH)
    scale = own_scale(ss)
    u = grad[...].astype(F32) * gain[...]
    xhat = joined[...].astype(F32) * scale
    out[...] = (scale * (u - xhat * c)).astype(BF16)


def over_half(copies):
    groups = [list(range(8)), list(range(8, 16))]
    return lax.all_to_all(copies, ("y", "c"), 0, 0, axis_index_groups=groups)


def transposed():
    return [(x * NY + y, (y // 2) * NY + 2 * x + y % 2) for x in range(NX) for y in range(NY)]


def shifted(value, k):
    return lax.ppermute(value, "x", [(i, (i + k) % NX) for i in range(NX)])


def kernel(body, name, outs, flops, specs, out_specs=None, scratch=(), limit=40):
    return pl.pallas_call(
        body,
        out_shape=tuple(jax.ShapeDtypeStruct(shape, dtype) for shape, dtype in outs),
        in_specs=specs,
        out_specs=out_specs or (VMEM,) * len(outs),
        scratch_shapes=scratch,
        compiler_params=pltpu.CompilerParams(vmem_limit_bytes=limit * MIB),
        cost_estimate=pl.CostEstimate(flops=flops, bytes_accessed=6 << 20, transcendentals=0),
        name=name,
    )


def per_device(joined, gain, weight_codes, scale_exp, cotangent):
    swap = [(0, 1), (1, 0)]
    flops = 2 * 1024 * WIDTH * WIDTH
    bricks, square, blocks, block = (NZ, ROWS, WIDTH), (WIDTH, WIDTH), (8, FEATS, COLS), (FEATS, WIDTH)
    gain = gain[None, :]
    joined_all = lax.all_gather(joined, "z")
    cot = lax.ppermute(cotangent.T, ("x", "y"), transposed())

    (weight,) = kernel(
        scaled_weight_kernel, "scaled_weight", (((NX,) + block, BF16),), 4 * FEATS * WIDTH, [VMEM] * 2
    )(weight_codes, scale_exp)
    weight = lax.all_to_all(weight, "x", 0, 0).reshape(square)

    own = lax.all_gather(cot, "y")
    other = lax.ppermute(own, "c", swap)

    scratch = [pltpu.VMEM((WIDTH, 1024), BF16), pltpu.VMEM(square, BF16), pltpu.VMEM(bricks, BF16), pltpu.SemaphoreType.DMA((17,))]
    (grad,) = kernel(
        input_grad_kernel,
        "input_grad",
        ((bricks, BF16),),
        flops,
        [ANY, ANY, VMEM, VMEM],
        scratch=[scratch[0], scratch[3]],
    )(own, other, weight, gain)
    grad = lax.psum_scatter(grad, "z")

    keep, send, squares = kernel(
        forward_kernel,
        "forward",
        ((blocks, BF16), (blocks, BF16), ((8, NZ, ROWS), F32)),
        flops,
        [VMEM] * 3,
        scratch=[scratch[1]],
    )(joined_all, gain, weight)
    got = lax.ppermute(send, "c", swap)
    squares = over_half(squares)

    mine, *others = kernel(
        weight_grad_kernel,
        "weight_grad",
        ((block, F32), (block, BF16), (block, BF16), (block, BF16)),
        flops,
        [VMEM, VMEM, ANY, ANY, ANY],
        scratch=[scratch[0], scratch[2], scratch[3]],
    )(squares, gain, own, other, joined_all)
    others = [shifted(other, k + 1) for k, other in enumerate(others)]

    (both,) = kernel(scale_kernel, "scale", ((blocks, BF16),), 4 * 8 * FEATS * COLS, [VMEM] * 3)(squares, keep, got)
    parts = lax.all_to_all(both, "y", 0, 0)
    projected = jnp.sum(parts.astype(F32), axis=0).astype(BF16)
    grad, projected = lax.optimization_barrier((grad, projected))
    dots, grad = kernel(
        dots_kernel, "dots", (((8, 1, ROWS), F32), ((ROWS, WIDTH), BF16)), 4 * ROWS * WIDTH, [VMEM] * 4
    )(squares, grad, joined, gain)
    projected = lax.ppermute(projected, ("x", "y"), transposed())
    dots = over_half(dots)
    joined_gradient, weight_grad, projected = kernel(
        last_kernel,
        "last",
        (((ROWS, WIDTH), BF16), (block, F32), ((FEATS, COLS), BF16)),
        8 * ROWS * WIDTH,
        [VMEM] * 10,
    )(squares, dots, grad, joined, gain, mine, *others, projected)
    return (projected.T, joined_gradient, weight_grad)


def solution(mesh):
    grid = Mesh(mesh.devices.reshape(NX, NZ, NY, NC), ("x", "z", "y", "c"))
    seq, tp = ("x", "z"), ("y", "c")
    in_specs = (P(seq, tp), P(tp), P(seq, tp), P(seq, tp), P(tp, seq))
    out_specs = (P(tp, seq), P(seq, tp), P(seq, tp))
    return jax.shard_map(per_device, mesh=grid, in_specs=in_specs, out_specs=out_specs, check_vma=False)
```
